512 devices in a mesh: blk: 256 (over y_lo, x, z, core), rep: 2 (over y_hi).
Axes of the slice: x: 4, y: 4 (y_hi: 2, y_lo: 2; y = y_hi * 2 + y_lo), z: 16, core: 2. Of those that a mesh axis runs over, the one named last changes fastest.
Arguments:
- audio_embed: bfloat16 [2, 65536, 1024], P('rep', 'blk'), may hold values from -0.25 to 0.25
- text_feats: bfloat16 [2, 65536, 768], P('rep', 'blk'), may hold values from -0.25 to 0.25
- text_head: bfloat16 [768, 1024], replicated, may hold values from -0.21875 to 0.21875
- pair_ids: int32 [2, 65536], P('rep', 'blk'), may hold values from 0 to 65535, as said below
- logit_scale: float32 [], replicated, may hold values from 2 to 8
- logit_bias: float32 [], replicated, may hold values from -3 to -1
Outputs:
- grad_audio_embed: bfloat16 [2, 65536, 1024], P('rep', 'blk')
- grad_text_feats: bfloat16 [2, 65536, 768], P('rep', 'blk')
- grad_text_head: bfloat16 [768, 1024], replicated
The draws below stay inside these ranges and needn't reach their ends.
Inputs may be any that keep to these rules, and one draw needn't show every extreme that they name: `pair_ids`: within every group and block, the pair ids of the block's 256 text rows are the row numbers of that same block's audio rows, each exactly once.
All inputs are finite; a program needn't handle non-finite values.
Results may differ from the reference program's by a relative error of at most 0.015.
Values may be sent and summed in bfloat16 or wider, within the bound.
No kernel may reach another device: no remote copies, remote signals or barrier semaphores. Data moves between devices by JAX's collectives and lax.ppermute only.
A program may use at most 64 MiB of HBM per device.

```python
import jax
import jax.numpy as jnp
from jax import lax

E = 1024
DT = 768
ROWS = 256
STEPS = 4
CYCLE_ROWS = 65536
N_REP = 2


def draw_pair_ids(key, part):
    key = jax.random.fold_in(key, 7)
    blocks = CYCLE_ROWS // ROWS
    keys = jax.random.split(key, N_REP * blocks)

    def one_block(block_key):
        return jax.random.permutation(block_key, ROWS).astype(jnp.int32)
    perms = jax.vmap(one_block)(keys).reshape(N_REP, blocks, ROWS)
    offsets = (jnp.arange(blocks, dtype=jnp.int32) * ROWS)[None, :, None]
    return (perms + offsets).reshape(N_REP, CYCLE_ROWS).astype(jnp.int32)


def shard_levels(rng, dims, pieces, low, high):
    factor_of, own = 1.0, jax.random.fold_in(rng, 6)
    for position, shards_of in pieces:
        draws = jnp.exp(jax.random.uniform(jax.random.fold_in(own, position), (shards_of,), jnp.float32, low / len(pieces), high / len(pieces)))
        factor_of = factor_of * jnp.repeat(draws, dims[position] // shards_of).reshape([-1 if axis == position else 1 for axis in range(len(dims))])
    return factor_of


def bell_draw(key, shape, deviation, most, cuts=(), held_as=jnp.bfloat16):
    result = jax.random.normal(key, shape, jnp.float32) * deviation
    if len(cuts) > 0:
        result = shard_levels(key, shape, cuts, -0.22, 0.18) * result
    return jnp.clip(result, min=-most, max=most).astype(held_as)


def setup_inputs(seed: int = 0) -> dict:
    key_of = jax.random.split(jax.random.key(seed), 7)
    audio_embed = bell_draw(key_of[0], (N_REP, CYCLE_ROWS, E), 0.03125, 0.25, ((0, 2), (1, 256)))
    text_feats = bell_draw(key_of[1], (N_REP, CYCLE_ROWS, DT), 0.03125, 0.25, ((0, 2), (1, 256)))
    text_head = bell_draw(key_of[2], (DT, E), DT ** -0.5, 0.21875)
    pair_ids = draw_pair_ids(jax.random.fold_in(key_of[6], 71), 0)
    logit_scale = jnp.clip(jax.random.uniform(key_of[4], (), jnp.float32, 2.0, 8.0), 2.0, 8.0)
    logit_bias = jnp.clip(jax.random.uniform(key_of[5], (), jnp.float32, -3.0, -1.0), -3.0, -1.0)
    return {"audio_embed": audio_embed, "text_feats": text_feats, "text_head": text_head, "pair_ids": pair_ids, "logit_scale": logit_scale, "logit_bias": logit_bias}


EPS = 1e-06

def unit_rows(values):
    wide = values.astype(jnp.float32)
    inverse = lax.rsqrt(lax.optimization_barrier(jnp.sum(wide * wide, axis=-1, keepdims=True)) + EPS)
    return (wide * inverse, inverse)

def one_group(audio, feats, ident, text_head, logit_scale, logit_bias):
    blocks = CYCLE_ROWS // ROWS
    audio_unit, audio_inv = unit_rows(audio)
    audio_b = audio_unit.astype(jnp.bfloat16)
    text_proj = jnp.dot(feats, text_head, preferred_element_type=jnp.float32)
    text_unit, text_inv = unit_rows(text_proj)
    text_b = text_unit.astype(jnp.bfloat16)
    audio_blk = audio_b.astype(jnp.float32).reshape(blocks, ROWS, E)
    text_blk = text_b.astype(jnp.float32).reshape(blocks, ROWS, E)
    owners = jnp.arange(blocks, dtype=jnp.int32)[:, None] * ROWS + jnp.arange(ROWS, dtype=jnp.int32)[None, :]
    ident_blk = ident.reshape(blocks, ROWS).astype(jnp.int32)
    positive = (owners[:, :, None] == ident_blk[:, None, :]).astype(jnp.float32)
    audio_grad = jnp.zeros((blocks, ROWS, E), jnp.float32)
    text_grad = jnp.zeros((blocks, ROWS, E), jnp.float32)
    for offset in range(STEPS):
        visiting = jnp.roll(text_blk, offset, axis=0)
        logits = logit_scale * jnp.einsum('bie,bje->bij', audio_blk, visiting) + logit_bias
        grads = jax.nn.sigmoid(logits)
        if offset == 0:
            grads = grads - positive
        weights = lax.optimization_barrier((logit_scale * grads).astype(jnp.bfloat16)).astype(jnp.float32)
        audio_grad = audio_grad + jnp.einsum('bij,bje->bie', weights, visiting)
        text_grad = text_grad + jnp.roll(jnp.einsum('bij,bie->bje', weights, audio_blk), -offset, axis=0)
    audio_grad = audio_grad.reshape(CYCLE_ROWS, E)
    text_grad = text_grad.reshape(CYCLE_ROWS, E)
    grad_audio = ((audio_grad - audio_unit * lax.optimization_barrier(jnp.sum(audio_unit * audio_grad, axis=-1, keepdims=True))) * audio_inv).astype(jnp.bfloat16)
    proj_grad = ((text_grad - text_unit * lax.optimization_barrier(jnp.sum(text_unit * text_grad, axis=-1, keepdims=True))) * text_inv).astype(jnp.bfloat16)
    grad_feats = jnp.dot(proj_grad, text_head.T, preferred_element_type=jnp.float32).astype(jnp.bfloat16)
    head_part = jnp.dot(feats.T, proj_grad, preferred_element_type=jnp.float32)
    return (grad_audio, grad_feats, head_part)

def reference(audio_embed, text_feats, text_head, pair_ids, logit_scale, logit_bias):
    audio_list = []
    feats_list = []
    head_total = jnp.zeros((DT, E), jnp.float32)
    for group in range(N_REP):
        grad_audio, grad_feats, head_part = one_group(audio_embed[group], text_feats[group], pair_ids[group], text_head, logit_scale, logit_bias)
        audio_list.append(grad_audio)
        feats_list.append(grad_feats)
        head_total = head_total + head_part
    return (jnp.stack(audio_list), jnp.stack(feats_list), head_total.astype(jnp.bfloat16))
```

```python
import jax
import jax.numpy as jnp
from jax import lax
from jax.sharding import Mesh, PartitionSpec as P

EPS = 1e-06
BLK = ("yl", "x", "z", "c")
PLANE = ("yl", "x", "yh")


def shifted(value, steps):
    count = lax.axis_size(BLK)
    return lax.ppermute(value, BLK, [(i, (i + steps) % count) for i in range(count)])


def other_core(value):
    return lax.ppermute(value, "c", [(0, 1), (1, 0)])


def even_odd(value, even, odd):
    count = lax.axis_size(BLK)
    return lax.ppermute(
        value, BLK, [(i, (i + (odd if i % 2 else even)) % count) for i in range(count)]
    )


def unit_rows(values):
    wide = values.astype(jnp.float32)
    inverse = lax.rsqrt(jnp.sum(wide * wide, axis=-1, keepdims=True) + EPS)
    return (wide * inverse, inverse)


def dot(a, b, da, db):
    return lax.dot_general(a, b, (((da,), (db,)), ((), ())), preferred_element_type=jnp.float32)


def pair_weights(audio_blk, text_blk, positive, scale, bias):
    grads = jax.nn.sigmoid(scale * dot(audio_blk, text_blk, 1, 1) + bias)
    if positive is not None:
        grads = grads - positive
    return (scale * grads).astype(jnp.bfloat16)


def body(audio_embed, text_feats, text_head, pair_ids, scale, bias):
    audio = audio_embed[0]
    feats = text_feats[0]
    ident = pair_ids[0]
    rows = audio.shape[0]
    core = lax.axis_index("c")
    first_row = lax.axis_index(BLK) * rows

    text_2 = shifted(feats, 2)
    audio_2 = shifted(audio, -2)
    text_a = even_odd(feats, 1, 3)
    audio_a = even_odd(audio, -3, -1)
    text_b = other_core(text_2)
    audio_b = other_core(audio_2)

    def project(block):
        unit, inv = unit_rows(jnp.dot(block, text_head, preferred_element_type=jnp.float32))
        return unit, inv, unit.astype(jnp.bfloat16)

    def audio_rows(block):
        return unit_rows(block)[0].astype(jnp.bfloat16)

    audio_unit, audio_inv = unit_rows(audio)
    own_audio = audio_unit.astype(jnp.bfloat16)
    text_unit, text_inv, own_text = project(feats)
    owners = first_row + lax.iota(jnp.int32, rows)
    positive = (owners[:, None] == ident[None, :]).astype(jnp.float32)
    weights = pair_weights(own_audio, own_text, positive, scale, bias)
    audio_grad = dot(weights, own_text, 1, 0)
    text_grad = dot(weights, own_audio, 0, 0)
    for block in (text_2, text_a, text_b):
        other = project(block)[2]
        audio_grad += dot(pair_weights(own_audio, other, None, scale, bias), other, 1, 0)
    for block in (audio_2, audio_a, audio_b):
        other = audio_rows(block)
        text_grad += dot(pair_weights(other, own_text, None, scale, bias), other, 0, 0)
    grad_audio = (
        (audio_grad - audio_unit * jnp.sum(audio_unit * audio_grad, axis=-1, keepdims=True))
        * audio_inv
    ).astype(jnp.bfloat16)
    proj_grad = (
        (text_grad - text_unit * jnp.sum(text_unit * text_grad, axis=-1, keepdims=True)) * text_inv
    ).astype(jnp.bfloat16)
    grad_feats = dot(proj_grad, text_head, 1, 1).astype(jnp.bfloat16)

    wide = proj_grad.shape[1]
    half = wide // 2
    mine = lax.dynamic_slice_in_dim(proj_grad, core * half, half, 1)
    theirs = lax.dynamic_slice_in_dim(proj_grad, (1 - core) * half, half, 1)
    sent = other_core(dot(feats, theirs, 0, 0).astype(jnp.bfloat16))
    part = (dot(feats, mine, 0, 0) + sent.astype(jnp.float32)).astype(jnp.bfloat16)
    plane = lax.axis_size(PLANE)
    depth = part.shape[0] // plane
    tiles = lax.all_to_all(part.reshape(plane, depth, half), PLANE, 0, 0, tiled=True)
    tile = jnp.sum(tiles.astype(jnp.float32), axis=0).astype(jnp.bfloat16)
    line = lax.all_gather(tile, "z", axis=0)
    total = jnp.sum(line.astype(jnp.float32), axis=0).astype(jnp.bfloat16)
    spread = lax.all_to_all(
        jnp.broadcast_to(total, (plane, depth, half)), PLANE, 0, 0, tiled=True
    ).reshape(plane * depth, half)
    other_half = other_core(spread)
    left = jnp.where(core == 0, spread, other_half)
    right = jnp.where(core == 0, other_half, spread)
    grad_head = jnp.concatenate([left, right], axis=1)
    return (grad_audio[None], grad_feats[None], grad_head)


def solution(mesh):
    fine = Mesh(mesh.devices.reshape(2, 4, 16, 2, 2), ("yl", "x", "z", "c", "yh"))
    rows = P("yh", BLK, None)
    return jax.shard_map(
        body,
        mesh=fine,
        in_specs=(rows, rows, P(), P("yh", BLK), P(), P()),
        out_specs=(rows, rows, P()),
        check_vma=False,
    )
```

```python
import jax
import jax.numpy as jnp
from jax import lax
from jax.experimental import pallas as pl
from jax.experimental.pallas import tpu as pltpu
from jax.sharding import Mesh, PartitionSpec as P

EPS = 1e-06
BLK = ("yl", "x", "zh", "zl", "c")
PLANE = ("yl", "x", "yh")
F32, BF16 = jnp.float32, jnp.bfloat16


def shifted(value, steps):
    count = lax.axis_size(BLK)
    return lax.ppermute(value, BLK, [(i, (i + steps) % count) for i in range(count)])


def other_core(value):
    return lax.ppermute(value, "c", [(0, 1), (1, 0)])


def tied(*values):
    return lax.optimization_barrier(values)


def unit_rows(wide):
    inverse = lax.rsqrt(jnp.sum(wide * wide, axis=-1, keepdims=True) + EPS)
    return (wide * inverse, inverse)


def dot(a, b, da, db):
    return lax.dot_general(a, b, (((da,), (db,)), ((), ())), preferred_element_type=F32)


def tangent(unit, inverse, grad):
    return (grad - unit * jnp.sum(unit * grad, axis=-1, keepdims=True)) * inverse


def sigmoids(left, right, scale, bias):
    return jax.nn.sigmoid(scale * dot(left, right, 1, 1) + bias)


def own_kernel(
    scale_ref, bias_ref, first_ref, audio_ref, feats_ref, head_ref, ident_ref,
    audio_b_ref, text_b_ref, unit_ref, inv_ref, audio_grad_ref, text_grad_ref, turned_ref,
):
    scale, bias = scale_ref[0], bias_ref[0]
    audio_b = unit_rows(audio_ref[...].astype(F32))[0].astype(BF16)
    unit, inverse = unit_rows(dot(feats_ref[...], head_ref[...], 1, 0))
    text_b = unit.astype(BF16)
    rows = audio_b.shape[0]
    owners = first_ref[0] + lax.broadcasted_iota(jnp.int32, (rows, rows), 0)
    positive = (owners == ident_ref[...]).astype(F32)
    weights = scale * (sigmoids(audio_b, text_b, scale, bias) - positive)
    audio_b_ref[...] = audio_b
    text_b_ref[...] = text_b
    unit_ref[...] = unit
    inv_ref[...] = inverse
    audio_grad_ref[...] = dot(weights.astype(BF16), text_b, 1, 0)
    text_grad_ref[...] = dot(weights.T.astype(BF16), audio_b, 1, 0)
    turned_ref[...] = feats_ref[...].T


def column_half(core, value):
    half = value.shape[1] // 2
    return jnp.where(core == 0, value[:, :half], value[:, half:])


def near_kernel(
    scale_ref, bias_ref, core_ref, audio_b_ref, text_b_ref, unit_ref, inv_ref, grad_ref, turned_ref,
    audio_1_ref, feats_2_ref, head_ref,
    proj_grad_ref, proj_grad_2_ref, turned_2_ref, theirs_ref, text_2_ref,
    weights_01_ref, weights_20_ref, weights_21_ref,
):
    scale, bias = scale_ref[0], bias_ref[0]
    audio_0, text_0 = audio_b_ref[...], text_b_ref[...]
    audio_1 = unit_rows(audio_1_ref[...].astype(F32))[0].astype(BF16)
    unit_2, inverse_2 = unit_rows(dot(feats_2_ref[...], head_ref[...], 1, 0))
    text_2 = unit_2.astype(BF16)
    weights_01 = (scale * sigmoids(text_0, audio_1, scale, bias)).astype(BF16)
    weights_20 = (scale * sigmoids(text_2, audio_0, scale, bias)).astype(BF16)
    weights_21 = (scale * sigmoids(text_2, audio_1, scale, bias)).astype(BF16)
    grad_0 = grad_ref[...] + dot(weights_01, audio_1, 1, 0)
    grad_2 = dot(weights_20, audio_0, 1, 0) + dot(weights_21, audio_1, 1, 0)
    proj_grad = tangent(unit_ref[...], inv_ref[...], grad_0).astype(BF16)
    proj_grad_2 = tangent(unit_2, inverse_2, grad_2).astype(BF16)
    turned_2 = feats_2_ref[...].T
    other = 1 - core_ref[0]
    theirs = dot(turned_ref[...], column_half(other, proj_grad), 1, 0)
    theirs += dot(turned_2, column_half(other, proj_grad_2), 1, 0)
    proj_grad_ref[...] = proj_grad
    proj_grad_2_ref[...] = proj_grad_2
    turned_2_ref[...] = turned_2
    theirs_ref[...] = theirs.astype(BF16)
    text_2_ref[...] = text_2
    weights_01_ref[...] = weights_01
    weights_20_ref[...] = weights_20
    weights_21_ref[...] = weights_21


def mine_kernel(core_ref, turned_ref, turned_2_ref, proj_grad_ref, proj_grad_2_ref, out_ref):
    out_ref[...] = dot(turned_ref[...], column_half(core_ref[0], proj_grad_ref[...]), 1, 0) + dot(
        turned_2_ref[...], column_half(core_ref[0], proj_grad_2_ref[...]), 1, 0
    )


def add_kernel(mine_ref, theirs_ref, out_ref):
    total = mine_ref[...] + theirs_ref[...].astype(F32)
    out_ref[...] = total.astype(BF16).reshape(out_ref.shape)


def back_kernel(
    audio_ref, audio_1_ref, grad_ref, text_0_ref, text_2_ref, weights_01_ref, weights_20_ref,
    weights_21_ref, proj_grad_2_ref, head_ref, kept_ref, back_1_ref, back_2_ref,
):
    text_0, text_2 = text_0_ref[...], text_2_ref[...]
    grad_0 = grad_ref[...] + dot(weights_20_ref[...], text_2, 0, 0)
    grad_1 = dot(weights_01_ref[...], text_0, 0, 0) + dot(weights_21_ref[...], text_2, 0, 0)
    kept_ref[...] = tangent(*unit_rows(audio_ref[...].astype(F32)), grad_0)
    back_1_ref[...] = tangent(*unit_rows(audio_1_ref[...].astype(F32)), grad_1).astype(BF16)
    back_2_ref[...] = dot(proj_grad_2_ref[...], head_ref[...], 1, 1).astype(BF16)


def finish_kernel(
    kept_ref, came_1_ref, proj_grad_ref, head_ref, came_2_ref, audio_out_ref, feats_out_ref
):
    audio_out_ref[...] = (kept_ref[...] + came_1_ref[...].astype(F32)).astype(BF16)
    feats = dot(proj_grad_ref[...], head_ref[...], 1, 1) + came_2_ref[...].astype(F32)
    feats_out_ref[...] = feats.astype(BF16)


def spread_kernel(tiles_ref, out_ref):
    total = jnp.sum(tiles_ref[...].astype(F32), axis=0).astype(BF16)
    out_ref[...] = jnp.broadcast_to(total[None], out_ref.shape)


def join_kernel(core_ref, mine_ref, theirs_ref, out_ref):
    half = mine_ref.shape[1]

    @pl.when(core_ref[0] == 0)
    def _():
        out_ref[:, :half] = mine_ref[...]
        out_ref[:, half:] = theirs_ref[...]

    @pl.when(core_ref[0] != 0)
    def _():
        out_ref[:, :half] = theirs_ref[...]
        out_ref[:, half:] = mine_ref[...]


def run(kernel, scalars, arrays, outs, macs):
    smem = pl.BlockSpec(memory_space=pltpu.SMEM)
    vmem = pl.BlockSpec(memory_space=pltpu.VMEM)
    moved = sum(a.size * a.dtype.itemsize for a in (*arrays, *outs))
    single = len(outs) == 1
    return pl.pallas_call(
        kernel,
        out_shape=outs[0] if single else outs,
        in_specs=[smem] * len(scalars) + [vmem] * len(arrays),
        out_specs=vmem if single else [vmem] * len(outs),
        compiler_params=pltpu.CompilerParams(vmem_limit_bytes=20 * 2**20),
        cost_estimate=pl.CostEstimate(flops=2 * macs, bytes_accessed=moved, transcendentals=0),
    )(*[s.reshape(1) for s in scalars], *arrays)


def shared_sum(tiles, copies):
    return run(spread_kernel, (), (tiles,), [jax.ShapeDtypeStruct((copies, *tiles.shape[1:]), BF16)], 0)


def body(audio_embed, text_feats, text_head, pair_ids, scale, bias):
    audio = audio_embed[0]
    feats = text_feats[0]
    rows, wide = audio.shape
    depth = feats.shape[1]
    half = wide // 2
    core = lax.axis_index("c")
    first_row = lax.axis_index(BLK) * rows
    shape = jax.ShapeDtypeStruct
    square, narrow = shape((rows, wide), BF16), shape((rows, depth), BF16)
    total, part_of = shape((rows, wide), F32), shape((depth, half), BF16)
    turned_of, weights_of = shape((depth, rows), BF16), shape((rows, rows), BF16)
    pair, project = rows * rows * wide, rows * wide * depth

    feats_2 = shifted(feats, 2)
    audio_1 = shifted(audio, -1)
    own_audio, own_text, unit, inverse, audio_grad, text_grad, turned = run(
        own_kernel,
        (scale, bias, first_row),
        (audio, feats, text_head, pair_ids),
        [square, square, total, shape((rows, 1), F32), total, total, turned_of],
        project + 3 * pair,
    )
    proj_grad, proj_grad_2, turned_2, theirs, text_2, *weights = run(
        near_kernel,
        (scale, bias, core),
        (own_audio, own_text, unit, inverse, text_grad, turned, audio_1, feats_2, text_head),
        [square, square, turned_of, part_of, square, weights_of, weights_of, weights_of],
        2 * project + 6 * pair,
    )

    theirs = other_core(theirs)
    mine = run(
        mine_kernel, (core,), (turned, turned_2, proj_grad, proj_grad_2),
        [shape((depth, half), F32)], project,
    )
    kept, back_1, back_2 = run(
        back_kernel, (),
        (audio, audio_1, audio_grad, own_text, text_2, *weights, proj_grad_2, text_head),
        [total, square, narrow], 3 * pair + project,
    )
    theirs, kept, back_1, back_2 = tied(theirs, kept, back_1, back_2)
    plane = lax.axis_size(PLANE)
    part = run(add_kernel, (), (mine, theirs), [shape((plane, depth // plane, half), BF16)], 0)
    part, back_1, back_2 = tied(part, back_1, back_2)
    came_2, came_1 = shifted(back_2, -2), shifted(back_1, 1)
    tiles = lax.all_to_all(part, PLANE, 0, 0, tiled=True)
    tile = shared_sum(tiles, lax.axis_size("zl"))
    came_1, came_2, tile = tied(came_1, came_2, tile)
    tiles = lax.all_to_all(tile, "zl", 0, 0, tiled=True)
    tile = shared_sum(tiles, lax.axis_size("zh"))
    tiles = lax.all_to_all(tile, "zh", 0, 0, tiled=True)
    spread = shared_sum(tiles, plane)
    spread = lax.all_to_all(spread, PLANE, 0, 0, tiled=True).reshape(depth, half)
    other_half = other_core(spread)
    came_1, spread = tied(came_1, spread)
    grad_audio, grad_feats = run(
        finish_kernel, (), (kept, came_1, proj_grad, text_head, came_2), [square, narrow], project
    )
    grad_head = run(join_kernel, (core,), (spread, other_half), [shape((depth, wide), BF16)], 0)
    return (grad_audio[None], grad_feats[None], grad_head)


def solution(mesh):
    fine = Mesh(mesh.devices.reshape(2, 4, 4, 4, 2, 2), ("yl", "x", "zh", "zl", "c", "yh"))
    rows = P("yh", BLK, None)
    return jax.shard_map(
        body,
        mesh=fine,
        in_specs=(rows, rows, P(), P("yh", BLK), P(), P()),
        out_specs=(rows, rows, P()),
        check_vma=False,
    )
```

```python
import jax
import jax.numpy as jnp
from jax import lax
from jax.experimental import pallas as pl
from jax.experimental.pallas import tpu as pltpu
from jax.sharding import Mesh, PartitionSpec as P

EPS = 1e-06
BLK = ("yl", "x", "zh", "zl", "c")
PLANE = ("yl", "x", "yh")
F32, BF16 = jnp.float32, jnp.bfloat16


def shifted(value, steps):
    count = lax.axis_size(BLK)
    return lax.ppermute(value, BLK, [(i, (i + steps) % count) for i in range(count)])


def other_core(value):
    return lax.ppermute(value, "c", [(0, 1), (1, 0)])


def tied(*values):
    return lax.optimization_barrier(values)


def unit_rows(wide):
    inverse = lax.rsqrt(jnp.sum(wide * wide, axis=-1, keepdims=True) + EPS)
    return (wide * inverse, inverse)


def dot(a, b, da, db):
    return lax.dot_general(a, b, (((da,), (db,)), ((), ())), preferred_element_type=F32)


def tangent(unit, inverse, grad):
    return (grad - unit * jnp.sum(unit * grad, axis=-1, keepdims=True)) * inverse


def sigmoids(left, right, scale, bias):
    return jax.nn.sigmoid(scale * dot(left, right, 1, 1) + bias)


def own_kernel(
    scale_ref, bias_ref, first_ref, audio_ref, feats_ref, head_ref, ident_ref,
    audio_b_ref, text_b_ref, unit_ref, inv_ref, text_grad_ref, turned_ref, audio_grad_hbm,
    audio_grad_ref, left,
):
    scale, bias = scale_ref[0], bias_ref[0]
    audio_b = unit_rows(audio_ref[...].astype(F32))[0].astype(BF16)
    unit, inverse = unit_rows(dot(feats_ref[...], head_ref[...], 1, 0))
    text_b = unit.astype(BF16)
    rows = audio_b.shape[0]
    owners = first_ref[0] + lax.broadcasted_iota(jnp.int32, (rows, rows), 0)
    positive = (owners == ident_ref[...]).astype(F32)
    weights = scale * (sigmoids(audio_b, text_b, scale, bias) - positive)
    audio_grad_ref[...] = dot(weights.astype(BF16), text_b, 1, 0)
    copy = pltpu.make_async_copy(audio_grad_ref, audio_grad_hbm, left.at[0])
    copy.start()
    audio_b_ref[...] = audio_b
    text_b_ref[...] = text_b
    unit_ref[...] = unit
    inv_ref[...] = inverse
    text_grad_ref[...] = dot(weights.T.astype(BF16), audio_b, 1, 0)
    turned_ref[...] = feats_ref[...].T
    copy.wait()


def column_half(core, value):
    half = value.shape[1] // 2
    return jnp.where(core == 0, value[:, :half], value[:, half:])


def audio_near_kernel(
    scale_ref, bias_ref, audio_1_ref, text_ref, unit_ref, inv_ref, grad_ref,
    audio_1_b_ref, proj_grad_ref, audio_grad_ref, proj_grad_hbm, kept_ref, left,
):
    text_b = text_ref[...]
    audio_1 = unit_rows(audio_1_ref[...].astype(F32))[0].astype(BF16)
    weights = scale_ref[0] * sigmoids(text_b, audio_1, scale_ref[0], bias_ref[0])
    grad = grad_ref[...] + dot(weights.astype(BF16), audio_1, 1, 0)
    proj_grad = tangent(unit_ref[...], inv_ref[...], grad).astype(BF16)
    proj_grad_ref[...] = proj_grad
    kept_ref[...] = proj_grad
    copy = pltpu.make_async_copy(kept_ref, proj_grad_hbm, left.at[0])
    copy.start()
    audio_1_b_ref[...] = audio_1
    audio_grad_ref[...] = dot(weights.T.astype(BF16), text_b, 1, 0)
    copy.wait()


def text_near_kernel(
    scale_ref, bias_ref, core_ref, feats_2_ref, head_ref, audio_0_ref, audio_1_ref,
    turned_ref, proj_grad_ref,
    text_2_ref, proj_grad_2_ref, turned_2_ref, theirs_ref, weights_21_ref,
    text_2_hbm, weights_20_hbm, text_kept_ref, weights_20_ref, left,
):
    scale, bias = scale_ref[0], bias_ref[0]
    audio_0, audio_1 = audio_0_ref[...], audio_1_ref[...]
    unit, inverse = unit_rows(dot(feats_2_ref[...], head_ref[...], 1, 0))
    text_2 = unit.astype(BF16)
    text_2_ref[...] = text_2
    text_kept_ref[...] = text_2
    first = pltpu.make_async_copy(text_kept_ref, text_2_hbm, left.at[0])
    first.start()
    weights_20 = (scale * sigmoids(text_2, audio_0, scale, bias)).astype(BF16)
    weights_20_ref[...] = weights_20
    second = pltpu.make_async_copy(weights_20_ref, weights_20_hbm, left.at[1])
    second.start()
    weights_21 = (scale * sigmoids(text_2, audio_1, scale, bias)).astype(BF16)
    grad = dot(weights_20, audio_0, 1, 0) + dot(weights_21, audio_1, 1, 0)
    proj_grad_2 = tangent(unit, inverse, grad).astype(BF16)
    turned_2 = feats_2_ref[...].T
    other = 1 - core_ref[0]
    theirs = dot(turned_ref[...], column_half(other, proj_grad_ref[...]), 1, 0)
    theirs += dot(turned_2, column_half(other, proj_grad_2), 1, 0)
    theirs_ref[...] = theirs.astype(BF16)
    proj_grad_2_ref[...] = proj_grad_2
    turned_2_ref[...] = turned_2
    weights_21_ref[...] = weights_21
    first.wait()
    second.wait()


def mine_kernel(core_ref, turned_0_ref, turned_2_ref, proj_grad_0_ref, proj_grad_2_ref, out_ref):
    out_ref[...] = dot(turned_0_ref[...], column_half(core_ref[0], proj_grad_0_ref[...]), 1, 0) + dot(
        turned_2_ref[...], column_half(core_ref[0], proj_grad_2_ref[...]), 1, 0
    )


def add_kernel(mine_ref, theirs_ref, out_ref):
    total = mine_ref[...] + theirs_ref[...].astype(F32)
    out_ref[...] = total.astype(BF16).reshape(out_ref.shape)


def back_kernel(
    audio_1_ref, text_2_ref, weights_21_ref, grad_ref, proj_grad_2_ref, head_ref,
    feats_hbm, audio_hbm, feats_ref, audio_ref, left,
):
    feats_ref[...] = dot(proj_grad_2_ref[...], head_ref[...], 1, 1).astype(BF16)
    first = pltpu.make_async_copy(feats_ref, feats_hbm, left.at[0])
    first.start()
    grad = grad_ref[...] + dot(weights_21_ref[...], text_2_ref[...], 0, 0)
    audio_ref[...] = tangent(*unit_rows(audio_1_ref[...].astype(F32)), grad).astype(BF16)
    second = pltpu.make_async_copy(audio_ref, audio_hbm, left.at[1])
    second.start()
    first.wait()
    second.wait()


def settle_kernel(
    audio_ref, grad_ref, weights_20_ref, text_2_ref, proj_grad_ref, head_ref, came_feats_ref,
    feats_out_ref, kept_hbm, kept_ref, left,
):
    grad = grad_ref[...] + dot(weights_20_ref[...], text_2_ref[...], 0, 0)
    kept_ref[...] = tangent(*unit_rows(audio_ref[...].astype(F32)), grad)
    copy = pltpu.make_async_copy(kept_ref, kept_hbm, left.at[0])
    copy.start()
    feats = dot(proj_grad_ref[...], head_ref[...], 1, 1) + came_feats_ref[...].astype(F32)
    feats_out_ref[...] = feats.astype(BF16)
    copy.wait()


def finish_kernel(kept_ref, came_audio_ref, out_ref):
    out_ref[...] = (kept_ref[...] + came_audio_ref[...].astype(F32)).astype(BF16)


def spread_kernel(tiles_ref, out_ref):
    total = jnp.sum(tiles_ref[...].astype(F32), axis=0).astype(BF16)
    out_ref[...] = jnp.broadcast_to(total[None], out_ref.shape)


def join_kernel(core_ref, mine_ref, theirs_ref, out_ref):
    half = mine_ref.shape[1]

    @pl.when(core_ref[0] == 0)
    def _():
        out_ref[:, :half] = mine_ref[...]
        out_ref[:, half:] = theirs_ref[...]

    @pl.when(core_ref[0] != 0)
    def _():
        out_ref[:, :half] = theirs_ref[...]
        out_ref[:, half:] = mine_ref[...]


def in_hbm(value):
    return pltpu.with_memory_space_constraint(value, pltpu.HBM)


def run(kernel, scalars, arrays, outs, macs, writes=0):
    smem = pl.BlockSpec(memory_space=pltpu.SMEM)
    vmem = pl.BlockSpec(memory_space=pltpu.VMEM)
    hbm = pl.BlockSpec(memory_space=pltpu.HBM)
    moved = sum(a.size * a.dtype.itemsize for a in (*arrays, *outs))
    single = len(outs) == 1
    kept = len(outs) - writes
    scratch = [pltpu.VMEM(a.shape, a.dtype) for a in outs[kept:]]
    if writes:
        scratch.append(pltpu.SemaphoreType.DMA((writes,)))
    outs = outs[:kept] + [pltpu.HBM(a.shape, a.dtype) for a in outs[kept:]]
    return pl.pallas_call(
        kernel,
        out_shape=outs[0] if single else outs,
        in_specs=[smem] * len(scalars) + [vmem] * len(arrays),
        out_specs=vmem if single else [vmem] * kept + [hbm] * writes,
        scratch_shapes=scratch,
        compiler_params=pltpu.CompilerParams(vmem_limit_bytes=20 * 2**20),
        cost_estimate=pl.CostEstimate(flops=2 * macs, bytes_accessed=moved, transcendentals=0),
    )(*[s.reshape(1) for s in scalars], *arrays)


def shared_sum(tiles, copies):
    return run(spread_kernel, (), (tiles,), [jax.ShapeDtypeStruct((copies, *tiles.shape[1:]), BF16)], 0)


def body(audio_embed, text_feats, text_head, pair_ids, scale, bias):
    audio = audio_embed[0]
    feats = text_feats[0]
    rows, wide = audio.shape
    depth = feats.shape[1]
    half = wide // 2
    core = lax.axis_index("c")
    first_row = lax.axis_index(BLK) * rows
    shape = jax.ShapeDtypeStruct
    square, narrow = shape((rows, wide), BF16), shape((rows, depth), BF16)
    total, part_of = shape((rows, wide), F32), shape((depth, half), BF16)
    turned_of, weights_of = shape((depth, rows), BF16), shape((rows, rows), BF16)
    pair, project = rows * rows * wide, rows * wide * depth

    feats_2 = shifted(feats, 2)
    audio_1 = shifted(audio, -1)
    own_audio, own_text, unit, inverse, text_grad, turned, audio_grad = run(
        own_kernel,
        (scale, bias, first_row),
        tuple(map(in_hbm, (audio, feats, text_head, pair_ids))),
        [square, square, total, shape((rows, 1), F32), total, turned_of, total],
        project + 3 * pair,
        writes=1,
    )
    audio_1_b, proj_grad, audio_1_grad, proj_grad_out = run(
        audio_near_kernel, (scale, bias), (audio_1, own_text, unit, inverse, text_grad),
        [square, square, total, square], 3 * pair, writes=1,
    )
    text_2, proj_grad_2, turned_2, theirs, weights_21, text_2_out, weights_20 = run(
        text_near_kernel, (scale, bias, core),
        (feats_2, text_head, own_audio, audio_1_b, turned, proj_grad),
        [square, square, turned_of, part_of, weights_of, square, weights_of],
        2 * project + 4 * pair, writes=2,
    )

    theirs = other_core(theirs)
    mine = run(
        mine_kernel, (core,), (turned, turned_2, proj_grad, proj_grad_2),
        [shape((depth, half), F32)], project,
    )
    back_feats, back_audio = run(
        back_kernel, (),
        (audio_1, text_2, weights_21, audio_1_grad, proj_grad_2, text_head),
        [narrow, square], pair + project, writes=2,
    )
    theirs, back_audio, back_feats = tied(theirs, back_audio, back_feats)
    plane = lax.axis_size(PLANE)
    part = run(add_kernel, (), (mine, theirs), [shape((plane, depth // plane, half), BF16)], 0)
    part, back_audio, back_feats = tied(part, back_audio, back_feats)
    came_audio, came_feats = shifted(back_audio, 1), shifted(back_feats, -2)
    tiles = lax.all_to_all(part, PLANE, 0, 0, tiled=True)
    tile = shared_sum(tiles, lax.axis_size("zl"))
    came_audio, came_feats, tile = tied(came_audio, came_feats, tile)
    tiles = lax.all_to_all(tile, "zl", 0, 0, tiled=True)
    tile = shared_sum(tiles, lax.axis_size("zh"))
    came_feats, tile = tied(came_feats, tile)
    grad_feats, kept = run(
        settle_kernel, (),
        tuple(map(in_hbm, (audio, audio_grad, weights_20, text_2_out, proj_grad_out, text_head,
                           came_feats))),
        [narrow, total], pair + project, writes=1,
    )
    tiles = lax.all_to_all(tile, "zh", 0, 0, tiled=True)
    tiles, grad_feats, kept = tied(tiles, grad_feats, kept)
    spread = shared_sum(tiles, plane)
    spread = lax.all_to_all(spread, PLANE, 0, 0, tiled=True).reshape(depth, half)
    other_half = other_core(spread)
    grad_audio = run(finish_kernel, (), (in_hbm(kept), in_hbm(came_audio)), [square], 0)
    grad_head = run(join_kernel, (core,), (spread, other_half), [shape((depth, wide), BF16)], 0)
    return (grad_audio[None], grad_feats[None], grad_head)


def solution(mesh):
    fine = Mesh(mesh.devices.reshape(2, 4, 4, 4, 2, 2), ("yl", "x", "zh", "zl", "c", "yh"))
    rows = P("yh", BLK, None)
    return jax.shard_map(
        body,
        mesh=fine,
        in_specs=(rows, rows, P(), P("yh", BLK), P(), P()),
        out_specs=(rows, rows, P()),
        check_vma=False,
    )
```

```python
import jax
import jax.numpy as jnp
from jax import lax
from jax.experimental import pallas as pl
from jax.experimental.pallas import tpu as pltpu
from jax.sharding import Mesh, PartitionSpec as P

EPS = 1e-06
BLK = ("yl", "x", "zh", "zl", "c")
PLANE = ("yl", "x", "yh")
F32, BF16 = jnp.float32, jnp.bfloat16


def shifted(value, steps):
    count = lax.axis_size(BLK)
    return lax.ppermute(value, BLK, [(i, (i + steps) % count) for i in range(count)])


def other_core(value):
    return lax.ppermute(value, "c", [(0, 1), (1, 0)])


def tied(*values):
    return lax.optimization_barrier(values)


def unit_rows(wide):
    inverse = lax.rsqrt(jnp.sum(wide * wide, axis=-1, keepdims=True) + EPS)
    return (wide * inverse, inverse)


def dot(a, b, da, db):
    return lax.dot_general(a, b, (((da,), (db,)), ((), ())), preferred_element_type=F32)


def tangent(unit, inverse, grad):
    return (grad - unit * jnp.sum(unit * grad, axis=-1, keepdims=True)) * inverse


def sigmoids(left, right, scale, bias):
    return jax.nn.sigmoid(scale * dot(left, right, 1, 1) + bias)


def own_kernel(
    scale_ref, bias_ref, first_ref, audio_ref, feats_ref, head_ref, ident_ref,
    audio_b_ref, text_b_ref, unit_ref, inv_ref, text_grad_ref, turned_ref, audio_grad_hbm,
    audio_grad_ref, left,
):
    scale, bias = scale_ref[0], bias_ref[0]
    audio_b = unit_rows(audio_ref[...].astype(F32))[0].astype(BF16)
    unit, inverse = unit_rows(dot(feats_ref[...], head_ref[...], 1, 0))
    text_b = unit.astype(BF16)
    rows = audio_b.shape[0]
    owners = first_ref[0] + lax.broadcasted_iota(jnp.int32, (rows, rows), 0)
    positive = (owners == ident_ref[...]).astype(F32)
    weights = scale * (sigmoids(audio_b, text_b, scale, bias) - positive)
    audio_grad_ref[...] = dot(weights.astype(BF16), text_b, 1, 0)
    copy = pltpu.make_async_copy(audio_grad_ref, audio_grad_hbm, left.at[0])
    copy.start()
    audio_b_ref[...] = audio_b
    text_b_ref[...] = text_b
    unit_ref[...] = unit
    inv_ref[...] = inverse
    text_grad_ref[...] = dot(weights.T.astype(BF16), audio_b, 1, 0)
    turned_ref[...] = feats_ref[...].T
    copy.wait()


def joined(low_ref, high_ref):
    return jnp.concatenate([low_ref[...], high_ref[...]], axis=1).astype(F32)


def column_half(core, value):
    half = value.shape[1] // 2
    return jnp.where(core == 0, value[:, :half], value[:, half:])


def audio_near_kernel(
    scale_ref, bias_ref, audio_1_ref, text_ref, unit_ref, inv_ref, grad_ref,
    audio_1_b_ref, proj_grad_ref, audio_grad_ref, proj_grad_hbm, kept_ref, left,
):
    text_b = text_ref[...]
    audio_1 = unit_rows(audio_1_ref[...].astype(F32))[0].astype(BF16)
    weights = scale_ref[0] * sigmoids(text_b, audio_1, scale_ref[0], bias_ref[0])
    grad = grad_ref[...] + dot(weights.astype(BF16), audio_1, 1, 0)
    proj_grad = tangent(unit_ref[...], inv_ref[...], grad).astype(BF16)
    proj_grad_ref[...] = proj_grad
    kept_ref[...] = proj_grad
    copy = pltpu.make_async_copy(kept_ref, proj_grad_hbm, left.at[0])
    copy.start()
    audio_1_b_ref[...] = audio_1
    audio_grad_ref[...] = dot(weights.T.astype(BF16), text_b, 1, 0)
    copy.wait()


def text_near_kernel(
    scale_ref, bias_ref, core_ref, feats_2_ref, head_ref, audio_0_ref, audio_1_ref,
    turned_ref, proj_grad_ref,
    text_2_ref, proj_grad_2_ref, turned_2_ref, theirs_ref, weights_21_ref,
    text_2_hbm, weights_20_hbm, text_kept_ref, weights_20_ref, left,
):
    scale, bias = scale_ref[0], bias_ref[0]
    audio_0, audio_1 = audio_0_ref[...], audio_1_ref[...]
    unit, inverse = unit_rows(dot(feats_2_ref[...], head_ref[...], 1, 0))
    text_2 = unit.astype(BF16)
    text_2_ref[...] = text_2
    text_kept_ref[...] = text_2
    first = pltpu.make_async_copy(text_kept_ref, text_2_hbm, left.at[0])
    first.start()
    weights_20 = (scale * sigmoids(text_2, audio_0, scale, bias)).astype(BF16)
    weights_20_ref[...] = weights_20
    second = pltpu.make_async_copy(weights_20_ref, weights_20_hbm, left.at[1])
    second.start()
    weights_21 = (scale * sigmoids(text_2, audio_1, scale, bias)).astype(BF16)
    grad = dot(weights_20, audio_0, 1, 0) + dot(weights_21, audio_1, 1, 0)
    proj_grad_2 = tangent(unit, inverse, grad).astype(BF16)
    turned_2 = feats_2_ref[...].T
    other = 1 - core_ref[0]
    theirs = dot(turned_ref[...], column_half(other, proj_grad_ref[...]), 1, 0)
    theirs += dot(turned_2, column_half(other, proj_grad_2), 1, 0)
    theirs_ref[...] = theirs.astype(BF16)
    proj_grad_2_ref[...] = proj_grad_2
    turned_2_ref[...] = turned_2
    weights_21_ref[...] = weights_21
    first.wait()
    second.wait()


def add_kernel(mine_ref, theirs_ref, out_ref):
    total = mine_ref[...] + theirs_ref[...].astype(F32)
    out_ref[...] = total.astype(BF16).reshape(out_ref.shape)


def back_kernel(
    core_ref, audio_1_ref, text_2_ref, weights_21_ref, grad_ref, head_ref,
    turned_ref, turned_2_ref, proj_grad_ref, proj_grad_2_ref,
    mine_ref, feats_hbm, low_hbm, high_hbm, feats_ref, low_ref, high_ref, left,
):
    proj_grad_2 = proj_grad_2_ref[...]
    feats_ref[...] = dot(proj_grad_2, head_ref[...], 1, 1).astype(BF16)
    first = pltpu.make_async_copy(feats_ref, feats_hbm, left.at[0])
    first.start()
    grad = grad_ref[...] + dot(weights_21_ref[...], text_2_ref[...], 0, 0)
    back = tangent(*unit_rows(audio_1_ref[...].astype(F32)), grad).astype(BF16)
    half = back.shape[1] // 2
    low_ref[...], high_ref[...] = back[:, :half], back[:, half:]
    second = pltpu.make_async_copy(low_ref, low_hbm, left.at[1])
    second.start()
    third = pltpu.make_async_copy(high_ref, high_hbm, left.at[2])
    third.start()
    mine = dot(turned_ref[...], column_half(core_ref[0], proj_grad_ref[...]), 1, 0)
    mine_ref[...] = mine + dot(turned_2_ref[...], column_half(core_ref[0], proj_grad_2), 1, 0)
    first.wait()
    second.wait()
    third.wait()


def settle_kernel(
    audio_ref, grad_ref, weights_20_ref, text_2_ref, came_low_ref, came_high_ref, proj_grad_ref,
    head_ref, came_feats_ref, audio_out_ref, feats_out_ref,
):
    grad = grad_ref[...] + dot(weights_20_ref[...], text_2_ref[...], 0, 0)
    kept = tangent(*unit_rows(audio_ref[...].astype(F32)), grad)
    audio_out_ref[...] = (kept + joined(came_low_ref, came_high_ref)).astype(BF16)
    feats = dot(proj_grad_ref[...], head_ref[...], 1, 1) + came_feats_ref[...].astype(F32)
    feats_out_ref[...] = feats.astype(BF16)


def spread_kernel(tiles_ref, out_ref):
    total = jnp.sum(tiles_ref[...].astype(F32), axis=0).astype(BF16)
    out_ref[...] = jnp.broadcast_to(total[None], out_ref.shape)


def join_kernel(core_ref, mine_ref, theirs_ref, out_ref):
    half = mine_ref.shape[1]

    @pl.when(core_ref[0] == 0)
    def _():
        out_ref[:, :half] = mine_ref[...]
        out_ref[:, half:] = theirs_ref[...]

    @pl.when(core_ref[0] != 0)
    def _():
        out_ref[:, :half] = theirs_ref[...]
        out_ref[:, half:] = mine_ref[...]


def in_hbm(value):
    return pltpu.with_memory_space_constraint(value, pltpu.HBM)


def run(kernel, scalars, arrays, outs, macs, writes=0):
    smem = pl.BlockSpec(memory_space=pltpu.SMEM)
    vmem = pl.BlockSpec(memory_space=pltpu.VMEM)
    hbm = pl.BlockSpec(memory_space=pltpu.HBM)
    moved = sum(a.size * a.dtype.itemsize for a in (*arrays, *outs))
    single = len(outs) == 1
    kept = len(outs) - writes
    scratch = [pltpu.VMEM(a.shape, a.dtype) for a in outs[kept:]]
    if writes:
        scratch.append(pltpu.SemaphoreType.DMA((writes,)))
    outs = outs[:kept] + [pltpu.HBM(a.shape, a.dtype) for a in outs[kept:]]
    return pl.pallas_call(
        kernel,
        out_shape=outs[0] if single else outs,
        in_specs=[smem] * len(scalars) + [vmem] * len(arrays),
        out_specs=vmem if single else [vmem] * kept + [hbm] * writes,
        scratch_shapes=scratch,
        compiler_params=pltpu.CompilerParams(vmem_limit_bytes=20 * 2**20),
        cost_estimate=pl.CostEstimate(flops=2 * macs, bytes_accessed=moved, transcendentals=0),
    )(*[s.reshape(1) for s in scalars], *arrays)


def shared_sum(tiles, copies):
    return run(spread_kernel, (), (tiles,), [jax.ShapeDtypeStruct((copies, *tiles.shape[1:]), BF16)], 0)


def body(audio_embed, text_feats, text_head, pair_ids, scale, bias):
    audio = audio_embed[0]
    feats = text_feats[0]
    rows, wide = audio.shape
    depth = feats.shape[1]
    half = wide // 2
    core = lax.axis_index("c")
    first_row = lax.axis_index(BLK) * rows
    shape = jax.ShapeDtypeStruct
    square, narrow = shape((rows, wide), BF16), shape((rows, depth), BF16)
    total, part_of = shape((rows, wide), F32), shape((depth, half), BF16)
    turned_of, weights_of = shape((depth, rows), BF16), shape((rows, rows), BF16)
    pair, project = rows * rows * wide, rows * wide * depth

    feats_2 = shifted(feats, 2)
    audio_1 = shifted(audio, -1)
    own_audio, own_text, unit, inverse, text_grad, turned, audio_grad = run(
        own_kernel,
        (scale, bias, first_row),
        tuple(map(in_hbm, (audio, feats, text_head, pair_ids))),
        [square, square, total, shape((rows, 1), F32), total, turned_of, total],
        project + 3 * pair,
        writes=1,
    )
    audio_1_b, proj_grad, audio_1_grad, proj_grad_out = run(
        audio_near_kernel, (scale, bias), (audio_1, own_text, unit, inverse, text_grad),
        [square, square, total, square], 3 * pair, writes=1,
    )
    text_2, proj_grad_2, turned_2, theirs, weights_21, text_2_out, weights_20 = run(
        text_near_kernel, (scale, bias, core),
        (feats_2, text_head, own_audio, audio_1_b, turned, proj_grad),
        [square, square, turned_of, part_of, weights_of, square, weights_of],
        2 * project + 4 * pair, writes=2,
    )

    theirs = other_core(theirs)
    mine, back_feats, *back_audio = run(
        back_kernel, (core,),
        (audio_1, text_2, weights_21, audio_1_grad, text_head, turned, turned_2, proj_grad,
         proj_grad_2),
        [shape((depth, half), F32), narrow, shape((rows, half), BF16), shape((rows, half), BF16)],
        pair + 2 * project, writes=3,
    )
    theirs, back_feats, *back_audio = tied(theirs, back_feats, *back_audio)
    plane = lax.axis_size(PLANE)
    part = run(add_kernel, (), (mine, theirs), [shape((plane, depth // plane, half), BF16)], 0)
    part, back_feats, *back_audio = tied(part, back_feats, *back_audio)
    came_feats = shifted(back_feats, -2)
    came_audio = [shifted(value, 1) for value in back_audio]
    tiles = lax.all_to_all(part, PLANE, 0, 0, tiled=True)
    tile = shared_sum(tiles, lax.axis_size("zl"))
    came_feats, tile, *came_audio = tied(came_feats, tile, *came_audio)
    tiles = lax.all_to_all(tile, "zl", 0, 0, tiled=True)
    tile = shared_sum(tiles, lax.axis_size("zh"))
    came_feats, tile = tied(came_feats, tile)
    grad_audio, grad_feats = run(
        settle_kernel, (),
        tuple(map(in_hbm, (audio, audio_grad, weights_20, text_2_out, *came_audio, proj_grad_out,
                           text_head, came_feats))),
        [square, narrow], pair + project,
    )
    tiles = lax.all_to_all(tile, "zh", 0, 0, tiled=True)
    tiles, grad_audio, grad_feats = tied(tiles, grad_audio, grad_feats)
    spread = shared_sum(tiles, plane)
    spread = lax.all_to_all(spread, PLANE, 0, 0, tiled=True).reshape(depth, half)
    grad_head = run(
        join_kernel, (core,), (spread, other_core(spread)), [shape((depth, wide), BF16)], 0
    )
    return (grad_audio[None], grad_feats[None], grad_head)


def solution(mesh):
    fine = Mesh(mesh.devices.reshape(2, 4, 4, 4, 2, 2), ("yl", "x", "zh", "zl", "c", "yh"))
    rows = P("yh", BLK, None)
    return jax.shard_map(
        body,
        mesh=fine,
        in_specs=(rows, rows, P(), P("yh", BLK), P(), P()),
        out_specs=(rows, rows, P()),
        check_vma=False,
    )
```

```python
import jax
import jax.numpy as jnp
from jax import lax
from jax.experimental import pallas as pl
from jax.experimental.pallas import tpu as pltpu
from jax.sharding import Mesh, PartitionSpec as P

EPS = 1e-06
BLK = ("yl", "x", "zh", "zl", "c")
PLANE = ("yl", "x", "yh")
F32, BF16 = jnp.float32, jnp.bfloat16


def shifted(value, steps):
    count = lax.axis_size(BLK)
    return lax.ppermute(value, BLK, [(i, (i + steps) % count) for i in range(count)])


def other_core(value):
    return lax.ppermute(value, "c", [(0, 1), (1, 0)])


def tied(*values):
    return lax.optimization_barrier(values)


def unit_rows(wide):
    inverse = lax.rsqrt(jnp.sum(wide * wide, axis=-1, keepdims=True) + EPS)
    return (wide * inverse, inverse)


def dot(a, b, da, db):
    return lax.dot_general(a, b, (((da,), (db,)), ((), ())), preferred_element_type=F32)


def tangent(unit, inverse, grad):
    return (grad - unit * jnp.sum(unit * grad, axis=-1, keepdims=True)) * inverse


def sigmoids(left, right, scale, bias):
    return jax.nn.sigmoid(scale * dot(left, right, 1, 1) + bias)


def own_kernel(
    scale_ref, bias_ref, first_ref, audio_ref, feats_ref, head_ref, ident_ref,
    audio_b_ref, text_b_ref, unit_ref, inv_ref, text_grad_ref, turned_ref, audio_grad_hbm,
    audio_grad_ref, left,
):
    scale, bias = scale_ref[0], bias_ref[0]
    audio_b = unit_rows(audio_ref[...].astype(F32))[0].astype(BF16)
    unit, inverse = unit_rows(dot(feats_ref[...], head_ref[...], 1, 0))
    text_b = unit.astype(BF16)
    rows = audio_b.shape[0]
    owners = first_ref[0] + lax.broadcasted_iota(jnp.int32, (rows, rows), 0)
    positive = (owners == ident_ref[...]).astype(F32)
    weights = scale * (sigmoids(audio_b, text_b, scale, bias) - positive)
    audio_grad_ref[...] = dot(weights.astype(BF16), text_b, 1, 0)
    copy = pltpu.make_async_copy(audio_grad_ref, audio_grad_hbm, left.at[0])
    copy.start()
    audio_b_ref[...] = audio_b
    text_b_ref[...] = text_b
    unit_ref[...] = unit
    inv_ref[...] = inverse
    text_grad_ref[...] = dot(weights.T.astype(BF16), audio_b, 1, 0)
    turned_ref[...] = feats_ref[...].T
    copy.wait()


def joined(low_ref, high_ref):
    return jnp.concatenate([low_ref[...], high_ref[...]], axis=1).astype(F32)


def column_half(core, value):
    half = value.shape[1] // 2
    return jnp.where(core == 0, value[:, :half], value[:, half:])


def audio_near_kernel(
    scale_ref, bias_ref, audio_1_ref, text_ref, unit_ref, inv_ref, grad_ref,
    audio_1_b_ref, proj_grad_ref, audio_grad_ref, proj_grad_hbm, kept_ref, left,
):
    text_b = text_ref[...]
    audio_1 = unit_rows(audio_1_ref[...].astype(F32))[0].astype(BF16)
    weights = scale_ref[0] * sigmoids(text_b, audio_1, scale_ref[0], bias_ref[0])
    grad = grad_ref[...] + dot(weights.astype(BF16), audio_1, 1, 0)
    proj_grad = tangent(unit_ref[...], inv_ref[...], grad).astype(BF16)
    proj_grad_ref[...] = proj_grad
    kept_ref[...] = proj_grad
    copy = pltpu.make_async_copy(kept_ref, proj_grad_hbm, left.at[0])
    copy.start()
    audio_1_b_ref[...] = audio_1
    audio_grad_ref[...] = dot(weights.T.astype(BF16), text_b, 1, 0)
    copy.wait()


def text_near_kernel(
    scale_ref, bias_ref, core_ref, feats_2_ref, head_ref, audio_0_ref, audio_1_ref,
    turned_ref, proj_grad_ref,
    text_2_ref, proj_grad_2_ref, turned_2_ref, theirs_ref, weights_21_ref,
    text_2_hbm, weights_20_hbm, text_kept_ref, weights_20_ref, left,
):
    scale, bias = scale_ref[0], bias_ref[0]
    audio_0, audio_1 = audio_0_ref[...], audio_1_ref[...]
    unit, inverse = unit_rows(dot(feats_2_ref[...], head_ref[...], 1, 0))
    text_2 = unit.astype(BF16)
    text_2_ref[...] = text_2
    text_kept_ref[...] = text_2
    first = pltpu.make_async_copy(text_kept_ref, text_2_hbm, left.at[0])
    first.start()
    weights_20 = (scale * sigmoids(text_2, audio_0, scale, bias)).astype(BF16)
    weights_20_ref[...] = weights_20
    second = pltpu.make_async_copy(weights_20_ref, weights_20_hbm, left.at[1])
    second.start()
    weights_21 = (scale * sigmoids(text_2, audio_1, scale, bias)).astype(BF16)
    grad = dot(weights_20, audio_0, 1, 0) + dot(weights_21, audio_1, 1, 0)
    proj_grad_2 = tangent(unit, inverse, grad).astype(BF16)
    turned_2 = feats_2_ref[...].T
    other = 1 - core_ref[0]
    theirs = dot(turned_ref[...], column_half(other, proj_grad_ref[...]), 1, 0)
    theirs += dot(turned_2, column_half(other, proj_grad_2), 1, 0)
    theirs_ref[...] = theirs.astype(BF16)
    proj_grad_2_ref[...] = proj_grad_2
    turned_2_ref[...] = turned_2
    weights_21_ref[...] = weights_21
    first.wait()
    second.wait()


def add_kernel(mine_ref, theirs_ref, out_ref):
    total = mine_ref[...] + theirs_ref[...].astype(F32)
    out_ref[...] = total.astype(BF16).reshape(out_ref.shape)


def back_kernel(
    core_ref, audio_1_ref, text_2_ref, weights_21_ref, grad_ref, head_ref,
    turned_ref, turned_2_ref, proj_grad_ref, proj_grad_2_ref,
    mine_ref, feats_hbm, low_hbm, high_hbm, feats_ref, low_ref, high_ref, left,
):
    proj_grad_2 = proj_grad_2_ref[...]
    feats_ref[...] = dot(proj_grad_2, head_ref[...], 1, 1).astype(BF16)
    first = pltpu.make_async_copy(feats_ref, feats_hbm, left.at[0])
    first.start()
    grad = grad_ref[...] + dot(weights_21_ref[...], text_2_ref[...], 0, 0)
    back = tangent(*unit_rows(audio_1_ref[...].astype(F32)), grad).astype(BF16)
    half = back.shape[1] // 2
    low_ref[...], high_ref[...] = back[:, :half], back[:, half:]
    second = pltpu.make_async_copy(low_ref, low_hbm, left.at[1])
    second.start()
    third = pltpu.make_async_copy(high_ref, high_hbm, left.at[2])
    third.start()
    mine = dot(turned_ref[...], column_half(core_ref[0], proj_grad_ref[...]), 1, 0)
    mine_ref[...] = mine + dot(turned_2_ref[...], column_half(core_ref[0], proj_grad_2), 1, 0)
    first.wait()
    second.wait()
    third.wait()


def settle_kernel(
    audio_ref, grad_ref, weights_20_ref, text_2_ref, came_low_ref, came_high_ref, proj_grad_ref,
    head_ref, came_feats_ref, audio_out_ref, feats_out_ref,
):
    grad = grad_ref[...] + dot(weights_20_ref[...], text_2_ref[...], 0, 0)
    kept = tangent(*unit_rows(audio_ref[...].astype(F32)), grad)
    audio_out_ref[...] = (kept + joined(came_low_ref, came_high_ref)).astype(BF16)
    feats = dot(proj_grad_ref[...], head_ref[...], 1, 1) + came_feats_ref[...].astype(F32)
    feats_out_ref[...] = feats.astype(BF16)


def spread_kernel(tiles_ref, out_ref):
    total = jnp.sum(tiles_ref[...].astype(F32), axis=0).astype(BF16)
    out_ref[...] = jnp.broadcast_to(total[None], out_ref.shape)


def join_kernel(core_ref, mine_ref, theirs_ref, out_ref):
    half = mine_ref.shape[1]

    @pl.when(core_ref[0] == 0)
    def _():
        out_ref[:, :half] = mine_ref[...]
        out_ref[:, half:] = theirs_ref[...]

    @pl.when(core_ref[0] != 0)
    def _():
        out_ref[:, :half] = theirs_ref[...]
        out_ref[:, half:] = mine_ref[...]


def in_hbm(value):
    return pltpu.with_memory_space_constraint(value, pltpu.HBM)


def run(kernel, scalars, arrays, outs, macs, writes=0):
    smem = pl.BlockSpec(memory_space=pltpu.SMEM)
    vmem = pl.BlockSpec(memory_space=pltpu.VMEM)
    hbm = pl.BlockSpec(memory_space=pltpu.HBM)
    moved = sum(a.size * a.dtype.itemsize for a in (*arrays, *outs))
    single = len(outs) == 1
    kept = len(outs) - writes
    scratch = [pltpu.VMEM(a.shape, a.dtype) for a in outs[kept:]]
    if writes:
        scratch.append(pltpu.SemaphoreType.DMA((writes,)))
    outs = outs[:kept] + [pltpu.HBM(a.shape, a.dtype) for a in outs[kept:]]
    return pl.pallas_call(
        kernel,
        out_shape=outs[0] if single else outs,
        in_specs=[smem] * len(scalars) + [vmem] * len(arrays),
        out_specs=vmem if single else [vmem] * kept + [hbm] * writes,
        scratch_shapes=scratch,
        compiler_params=pltpu.CompilerParams(vmem_limit_bytes=20 * 2**20),
        cost_estimate=pl.CostEstimate(flops=2 * macs, bytes_accessed=moved, transcendentals=0),
    )(*[s.reshape(1) for s in scalars], *arrays)


def shared_sum(tiles, copies):
    return run(spread_kernel, (), (tiles,), [jax.ShapeDtypeStruct((copies, *tiles.shape[1:]), BF16)], 0)


def body(audio_embed, text_feats, text_head, pair_ids, scale, bias):
    audio = audio_embed[0]
    feats = text_feats[0]
    rows, wide = audio.shape
    depth = feats.shape[1]
    half = wide // 2
    core = lax.axis_index("c")
    first_row = lax.axis_index(BLK) * rows
    shape = jax.ShapeDtypeStruct
    square, narrow = shape((rows, wide), BF16), shape((rows, depth), BF16)
    total, part_of = shape((rows, wide), F32), shape((depth, half), BF16)
    turned_of, weights_of = shape((depth, rows), BF16), shape((rows, rows), BF16)
    pair, project = rows * rows * wide, rows * wide * depth

    feats_2 = shifted(feats, 2)
    audio_1 = shifted(audio, -1)
    own_audio, own_text, unit, inverse, text_grad, turned, audio_grad = run(
        own_kernel,
        (scale, bias, first_row),
        tuple(map(in_hbm, (audio, feats, text_head, pair_ids))),
        [square, square, total, shape((rows, 1), F32), total, turned_of, total],
        project + 3 * pair,
        writes=1,
    )
    audio_1_b, proj_grad, audio_1_grad, proj_grad_out = run(
        audio_near_kernel, (scale, bias), (audio_1, own_text, unit, inverse, text_grad),
        [square, square, total, square], 3 * pair, writes=1,
    )
    text_2, proj_grad_2, turned_2, theirs, weights_21, text_2_out, weights_20 = run(
        text_near_kernel, (scale, bias, core),
        (feats_2, text_head, own_audio, audio_1_b, turned, proj_grad),
        [square, square, turned_of, part_of, weights_of, square, weights_of],
        2 * project + 4 * pair, writes=2,
    )

    theirs = other_core(theirs)
    mine, back_feats, *back_audio = run(
        back_kernel, (core,),
        (audio_1, text_2, weights_21, audio_1_grad, text_head, turned, turned_2, proj_grad,
         proj_grad_2),
        [shape((depth, half), F32), narrow, shape((rows, half), BF16), shape((rows, half), BF16)],
        pair + 2 * project, writes=3,
    )
    theirs, back_feats, *back_audio = tied(theirs, back_feats, *back_audio)
    plane = lax.axis_size(PLANE)
    part = run(add_kernel, (), (mine, theirs), [shape((plane, depth // plane, half), BF16)], 0)
    part, back_feats, *back_audio = tied(part, back_feats, *back_audio)
    came_feats = shifted(back_feats, -2)
    came_audio = [shifted(value, 1) for value in back_audio]
    tiles = lax.all_to_all(part, PLANE, 0, 0, tiled=True)
    tile = shared_sum(tiles, lax.axis_size("zh"))
    came_feats, tile, *came_audio = tied(came_feats, tile, *came_audio)
    tiles = lax.all_to_all(tile, "zh", 0, 0, tiled=True)
    tile = shared_sum(tiles, lax.axis_size("zl"))
    came_feats, tile = tied(came_feats, tile)
    grad_audio, grad_feats = run(
        settle_kernel, (),
        tuple(map(in_hbm, (audio, audio_grad, weights_20, text_2_out, *came_audio, proj_grad_out,
                           text_head, came_feats))),
        [square, narrow], pair + project,
    )
    tiles = lax.all_to_all(tile, "zl", 0, 0, tiled=True)
    tiles, grad_audio, grad_feats = tied(tiles, grad_audio, grad_feats)
    spread = shared_sum(tiles, plane)
    spread = lax.all_to_all(spread, PLANE, 0, 0, tiled=True).reshape(depth, half)
    grad_head = run(
        join_kernel, (core,), (spread, other_core(spread)), [shape((depth, wide), BF16)], 0
    )
    return (grad_audio[None], grad_feats[None], grad_head)


def solution(mesh):
    fine = Mesh(mesh.devices.reshape(2, 4, 4, 4, 2, 2), ("yl", "x", "zh", "zl", "c", "yh"))
    rows = P("yh", BLK, None)
    return jax.shard_map(
        body,
        mesh=fine,
        in_specs=(rows, rows, P(), P("yh", BLK), P(), P()),
        out_specs=(rows, rows, P()),
        check_vma=False,
    )
```

```python
import jax
import jax.numpy as jnp
from jax import lax
from jax.experimental import pallas as pl
from jax.experimental.pallas import tpu as pltpu
from jax.sharding import Mesh, PartitionSpec as P

EPS = 1e-06
BLK = ("yl", "x", "zh", "zl", "c")
PLANE = ("yl", "x", "yh")
F32, BF16 = jnp.float32, jnp.bfloat16


def shifted(value, steps):
    count = lax.axis_size(BLK)
    return lax.ppermute(value, BLK, [(i, (i + steps) % count) for i in range(count)])


def other_core(value):
    return lax.ppermute(value, "c", [(0, 1), (1, 0)])


def tied(*values):
    return lax.optimization_barrier(values)


def unit_rows(wide):
    inverse = lax.rsqrt(jnp.sum(wide * wide, axis=-1, keepdims=True) + EPS)
    return (wide * inverse, inverse)


def dot(a, b, da, db):
    return lax.dot_general(a, b, (((da,), (db,)), ((), ())), preferred_element_type=F32)


def tangent(unit, inverse, grad):
    return (grad - unit * jnp.sum(unit * grad, axis=-1, keepdims=True)) * inverse


def sigmoids(left, right, scale, bias):
    return jax.nn.sigmoid(scale * dot(left, right, 1, 1) + bias)


def own_kernel(
    scale_ref, bias_ref, first_ref, audio_ref, feats_ref, head_ref, ident_ref,
    audio_b_ref, text_b_ref, unit_ref, inv_ref, text_grad_ref, turned_ref, audio_grad_hbm,
    audio_grad_ref, left,
):
    scale, bias = scale_ref[0], bias_ref[0]
    audio_b = unit_rows(audio_ref[...].astype(F32))[0].astype(BF16)
    unit, inverse = unit_rows(dot(feats_ref[...], head_ref[...], 1, 0))
    text_b = unit.astype(BF16)
    rows = audio_b.shape[0]
    owners = first_ref[0] + lax.broadcasted_iota(jnp.int32, (rows, rows), 0)
    positive = (owners == ident_ref[...]).astype(F32)
    weights = scale * (sigmoids(audio_b, text_b, scale, bias) - positive)
    audio_grad_ref[...] = dot(weights.astype(BF16), text_b, 1, 0)
    copy = pltpu.make_async_copy(audio_grad_ref, audio_grad_hbm, left.at[0])
    copy.start()
    audio_b_ref[...] = audio_b
    text_b_ref[...] = text_b
    unit_ref[...] = unit
    inv_ref[...] = inverse
    text_grad_ref[...] = dot(weights.T.astype(BF16), audio_b, 1, 0)
    turned_ref[...] = feats_ref[...].T
    copy.wait()


def joined(low_ref, high_ref):
    return jnp.concatenate([low_ref[...], high_ref[...]], axis=1).astype(F32)


def column_half(core, value):
    half = value.shape[1] // 2
    return jnp.where(core == 0, value[:, :half], value[:, half:])


def audio_near_kernel(
    scale_ref, bias_ref, audio_1_ref, text_ref, unit_ref, inv_ref, grad_ref,
    audio_1_b_ref, proj_grad_ref, audio_grad_ref, proj_grad_hbm, kept_ref, left,
):
    text_b = text_ref[...]
    audio_1 = unit_rows(audio_1_ref[...].astype(F32))[0].astype(BF16)
    weights = scale_ref[0] * sigmoids(text_b, audio_1, scale_ref[0], bias_ref[0])
    grad = grad_ref[...] + dot(weights.astype(BF16), audio_1, 1, 0)
    proj_grad = tangent(unit_ref[...], inv_ref[...], grad).astype(BF16)
    proj_grad_ref[...] = proj_grad
    kept_ref[...] = proj_grad
    copy = pltpu.make_async_copy(kept_ref, proj_grad_hbm, left.at[0])
    copy.start()
    audio_1_b_ref[...] = audio_1
    audio_grad_ref[...] = dot(weights.T.astype(BF16), text_b, 1, 0)
    copy.wait()


def text_near_kernel(
    scale_ref, bias_ref, core_ref, feats_2_ref, head_ref, audio_0_ref, audio_1_ref,
    turned_ref, proj_grad_ref,
    text_2_ref, proj_grad_2_ref, turned_2_ref, theirs_ref, weights_21_ref,
    text_2_hbm, weights_20_hbm, text_kept_ref, weights_20_ref, left,
):
    scale, bias = scale_ref[0], bias_ref[0]
    audio_0, audio_1 = audio_0_ref[...], audio_1_ref[...]
    unit, inverse = unit_rows(dot(feats_2_ref[...], head_ref[...], 1, 0))
    text_2 = unit.astype(BF16)
    text_2_ref[...] = text_2
    text_kept_ref[...] = text_2
    first = pltpu.make_async_copy(text_kept_ref, text_2_hbm, left.at[0])
    first.start()
    weights_20 = (scale * sigmoids(text_2, audio_0, scale, bias)).astype(BF16)
    weights_20_ref[...] = weights_20
    second = pltpu.make_async_copy(weights_20_ref, weights_20_hbm, left.at[1])
    second.start()
    weights_21 = (scale * sigmoids(text_2, audio_1, scale, bias)).astype(BF16)
    grad = dot(weights_20, audio_0, 1, 0) + dot(weights_21, audio_1, 1, 0)
    proj_grad_2 = tangent(unit, inverse, grad).astype(BF16)
    turned_2 = feats_2_ref[...].T
    other = 1 - core_ref[0]
    theirs = dot(turned_ref[...], column_half(other, proj_grad_ref[...]), 1, 0)
    theirs += dot(turned_2, column_half(other, proj_grad_2), 1, 0)
    theirs_ref[...] = theirs.astype(BF16)
    proj_grad_2_ref[...] = proj_grad_2
    turned_2_ref[...] = turned_2
    weights_21_ref[...] = weights_21
    first.wait()
    second.wait()


def add_kernel(mine_ref, theirs_ref, out_hbm, out_ref, left):
    tiles, depth, width = out_ref.shape
    chunk, copies = tiles // 4, []
    for i in range(4):
        rows = slice(i * chunk * depth, (i + 1) * chunk * depth)
        total = mine_ref[rows, :] + theirs_ref[rows, :].astype(F32)
        out_ref[i * chunk : (i + 1) * chunk] = total.astype(BF16).reshape(chunk, depth, width)
        part = pl.ds(i * chunk, chunk)
        copies.append(pltpu.make_async_copy(out_ref.at[part], out_hbm.at[part], left.at[i]))
        copies[-1].start()
    for copy in copies:
        copy.wait()


def back_kernel(
    core_ref, audio_1_ref, text_2_ref, weights_21_ref, grad_ref, head_ref,
    turned_ref, turned_2_ref, proj_grad_ref, proj_grad_2_ref,
    mine_ref, feats_hbm, low_hbm, high_hbm, feats_ref, low_ref, high_ref, left,
):
    proj_grad_2 = proj_grad_2_ref[...]
    feats_ref[...] = dot(proj_grad_2, head_ref[...], 1, 1).astype(BF16)
    first = pltpu.make_async_copy(feats_ref, feats_hbm, left.at[0])
    first.start()
    grad = grad_ref[...] + dot(weights_21_ref[...], text_2_ref[...], 0, 0)
    back = tangent(*unit_rows(audio_1_ref[...].astype(F32)), grad).astype(BF16)
    half = back.shape[1] // 2
    low_ref[...], high_ref[...] = back[:, :half], back[:, half:]
    second = pltpu.make_async_copy(low_ref, low_hbm, left.at[1])
    second.start()
    third = pltpu.make_async_copy(high_ref, high_hbm, left.at[2])
    third.start()
    mine = dot(turned_ref[...], column_half(core_ref[0], proj_grad_ref[...]), 1, 0)
    mine_ref[...] = mine + dot(turned_2_ref[...], column_half(core_ref[0], proj_grad_2), 1, 0)
    first.wait()
    second.wait()
    third.wait()


def settle_kernel(
    audio_ref, grad_ref, weights_20_ref, text_2_ref, came_low_ref, came_high_ref, proj_grad_ref,
    head_ref, came_feats_ref, audio_out_ref, feats_out_ref,
):
    grad = grad_ref[...] + dot(weights_20_ref[...], text_2_ref[...], 0, 0)
    kept = tangent(*unit_rows(audio_ref[...].astype(F32)), grad)
    audio_out_ref[...] = (kept + joined(came_low_ref, came_high_ref)).astype(BF16)
    feats = dot(proj_grad_ref[...], head_ref[...], 1, 1) + came_feats_ref[...].astype(F32)
    feats_out_ref[...] = feats.astype(BF16)


def spread_kernel(tiles_ref, out_ref):
    total = jnp.sum(tiles_ref[...].astype(F32), axis=0).astype(BF16)
    out_ref[...] = jnp.broadcast_to(total[None], out_ref.shape)


def join_kernel(core_ref, mine_ref, theirs_ref, out_ref):
    half = mine_ref.shape[1]

    @pl.when(core_ref[0] == 0)
    def _():
        out_ref[:, :half] = mine_ref[...]
        out_ref[:, half:] = theirs_ref[...]

    @pl.when(core_ref[0] != 0)
    def _():
        out_ref[:, :half] = theirs_ref[...]
        out_ref[:, half:] = mine_ref[...]


def in_hbm(value):
    return pltpu.with_memory_space_constraint(value, pltpu.HBM)


def run(kernel, scalars, arrays, outs, macs, writes=0):
    smem = pl.BlockSpec(memory_space=pltpu.SMEM)
    vmem = pl.BlockSpec(memory_space=pltpu.VMEM)
    hbm = pl.BlockSpec(memory_space=pltpu.HBM)
    moved = sum(a.size * a.dtype.itemsize for a in (*arrays, *outs))
    single = len(outs) == 1
    kept = len(outs) - writes
    scratch = [pltpu.VMEM(a.shape, a.dtype) for a in outs[kept:]]
    if writes:
        scratch.append(pltpu.SemaphoreType.DMA((max(writes, 4),)))
    outs = outs[:kept] + [pltpu.HBM(a.shape, a.dtype) for a in outs[kept:]]
    return pl.pallas_call(
        kernel,
        out_shape=outs[0] if single else outs,
        in_specs=[smem] * len(scalars) + [vmem] * len(arrays),
        out_specs=vmem if single else [vmem] * kept + [hbm] * writes,
        scratch_shapes=scratch,
        compiler_params=pltpu.CompilerParams(vmem_limit_bytes=20 * 2**20),
        cost_estimate=pl.CostEstimate(flops=2 * macs, bytes_accessed=moved, transcendentals=0),
    )(*[s.reshape(1) for s in scalars], *arrays)


def shared_sum(tiles, copies):
    return run(spread_kernel, (), (tiles,), [jax.ShapeDtypeStruct((copies, *tiles.shape[1:]), BF16)], 0)


def body(audio_embed, text_feats, text_head, pair_ids, scale, bias):
    audio = audio_embed[0]
    feats = text_feats[0]
    rows, wide = audio.shape
    depth = feats.shape[1]
    half = wide // 2
    core = lax.axis_index("c")
    first_row = lax.axis_index(BLK) * rows
    shape = jax.ShapeDtypeStruct
    square, narrow = shape((rows, wide), BF16), shape((rows, depth), BF16)
    total, part_of = shape((rows, wide), F32), shape((depth, half), BF16)
    turned_of, weights_of = shape((depth, rows), BF16), shape((rows, rows), BF16)
    pair, project = rows * rows * wide, rows * wide * depth

    feats_2 = shifted(feats, 2)
    audio_1 = shifted(audio, -1)
    own_audio, own_text, unit, inverse, text_grad, turned, audio_grad = run(
        own_kernel,
        (scale, bias, first_row),
        tuple(map(in_hbm, (audio, feats, text_head, pair_ids))),
        [square, square, total, shape((rows, 1), F32), total, turned_of, total],
        project + 3 * pair,
        writes=1,
    )
    audio_1_b, proj_grad, audio_1_grad, proj_grad_out = run(
        audio_near_kernel, (scale, bias), (audio_1, own_text, unit, inverse, text_grad),
        [square, square, total, square], 3 * pair, writes=1,
    )
    text_2, proj_grad_2, turned_2, theirs, weights_21, text_2_out, weights_20 = run(
        text_near_kernel, (scale, bias, core),
        (feats_2, text_head, own_audio, audio_1_b, turned, proj_grad),
        [square, square, turned_of, part_of, weights_of, square, weights_of],
        2 * project + 4 * pair, writes=2,
    )

    theirs = other_core(theirs)
    mine, back_feats, *back_audio = run(
        back_kernel, (core,),
        (audio_1, text_2, weights_21, audio_1_grad, text_head, turned, turned_2, proj_grad,
         proj_grad_2),
        [shape((depth, half), F32), narrow, shape((rows, half), BF16), shape((rows, half), BF16)],
        pair + 2 * project, writes=3,
    )
    theirs, back_feats, *back_audio = tied(theirs, back_feats, *back_audio)
    plane = lax.axis_size(PLANE)
    part = run(
        add_kernel, (), (mine, theirs), [shape((plane, depth // plane, half), BF16)], 0, writes=1
    )
    part, back_feats, *back_audio = tied(part, back_feats, *back_audio)
    came_feats = shifted(back_feats, -2)
    came_audio = [shifted(value, 1) for value in back_audio]
    tiles = lax.all_to_all(part, PLANE, 0, 0, tiled=True)
    tile = shared_sum(tiles, lax.axis_size("zh"))
    came_feats, tile, *came_audio = tied(came_feats, tile, *came_audio)
    tiles = lax.all_to_all(tile, "zh", 0, 0, tiled=True)
    tile = shared_sum(tiles, lax.axis_size("zl"))
    came_feats, tile = tied(came_feats, tile)
    grad_audio, grad_feats = run(
        settle_kernel, (),
        tuple(map(in_hbm, (audio, audio_grad, weights_20, text_2_out, *came_audio, proj_grad_out,
                           text_head, came_feats))),
        [square, narrow], pair + project,
    )
    tiles = lax.all_to_all(tile, "zl", 0, 0, tiled=True)
    tiles, grad_audio, grad_feats = tied(tiles, grad_audio, grad_feats)
    spread = shared_sum(tiles, plane)
    spread = lax.all_to_all(spread, PLANE, 0, 0, tiled=True).reshape(depth, half)
    grad_head = run(
        join_kernel, (core,), (spread, other_core(spread)), [shape((depth, wide), BF16)], 0
    )
    return (grad_audio[None], grad_feats[None], grad_head)


def solution(mesh):
    fine = Mesh(mesh.devices.reshape(2, 4, 4, 4, 2, 2), ("yl", "x", "zh", "zl", "c", "yh"))
    rows = P("yh", BLK, None)
    return jax.shard_map(
        body,
        mesh=fine,
        in_specs=(rows, rows, P(), P("yh", BLK), P(), P()),
        out_specs=(rows, rows, P()),
        check_vma=False,
    )
```
